32 devices in a mesh: groups: 2 (over y), tok: 4 (over z), mp: 2 (over x), sub: 2 (over core).
Axes of the slice: x: 2, y: 2, z: 4, core: 2. Of those that a mesh axis runs over, the one named last changes fastest.
Arguments:
- inputs: bfloat16 [12288, 5120], P(('groups', 'tok'), ('mp', 'sub')), parts along dimension 0, may hold values from -6 to 6
- base_weight: bfloat16 [5120, 2048], P(('mp', 'sub')), may hold values from -0.078125 to 0.078125
- panel_a: bfloat16 [256, 64, 5120], P(('groups', 'tok'), None, ('mp', 'sub')), parts along dimension 0, may hold values from -0.078125 to 0.078125
- panel_b: bfloat16 [256, 64, 2048], P(('groups', 'tok'), None, ('mp', 'sub')), parts along dimension 0, may hold values from -0.75 to 0.75
- teacher: bfloat16 [12288, 2048], P(('groups', 'tok'), ('mp', 'sub')), parts along dimension 0, may hold values from -6 to 6
- block_ids: int32 [8, 12], P('groups'), parts along dimension 0, may hold values from 0 to 127, as said below
- home_rows: int32 [256], P('groups'), parts along dimension 0, may hold values from 0 to 127, as said below
- live_blocks: int32 [8], P('groups'), parts along dimension 0, may hold values from 1 to 12, 28 in all
Outputs:
- grad_a: bfloat16 [256, 64, 5120], P(('groups', 'tok'), None, ('mp', 'sub')), parts along dimension 0
- grad_b: bfloat16 [256, 64, 2048], P(('groups', 'tok'), None, ('mp', 'sub')), parts along dimension 0
The draws below stay inside these ranges and needn't reach their ends.
There are 2 independent parts, one for each index of `groups`. The reference program is written for one: setup_inputs(seed, part) draws one part's arguments, and reference() takes and returns one part's arrays. A program takes and returns all parts, laid end to end along the dimension named above; an argument that names none is the same for every part. Nothing has to cross between parts.
Inputs may be any that keep to these rules, and one draw needn't show every extreme that they name: A permutation: adapter a is stored at row home_rows[a], on tok index home_rows[a] // 32. `block_ids`: adapter ids. Among the 12 blocks of one tok index at most 6 use adapters stored on one tok index, and on every tok index some storing index serves exactly 6 of them.
All inputs are finite; a program needn't handle non-finite values.
Results may differ from the reference program's by a relative error of at most 0.017.
Values may be sent and summed in bfloat16 or wider, within the bound.
A program may use at most 128 MiB of HBM per device.

```python
import math
import jax
import jax.numpy as jnp
import numpy as np
from jax import lax

D = 5120
KV = 1024
R = 64
BLK = 128
BLK_DEV = 12
ADP_DEV = 32
CAP = 6
TOKENS = 6144
ADAPTERS = 128
N_TOK = 4
N_MP = 2
N_SUB = 2


def draw_layout(key):
    return jax.random.permutation(key, ADAPTERS)


def draw_home_rows(key, part):
    return draw_layout(key).astype(jnp.int32)


def draw_block_ids(key, part):
    slot_order = draw_layout(key)
    inverse = jnp.argsort(slot_order)
    key = jax.random.fold_in(key, 11)
    device_keys = jax.random.split(key, N_TOK)

    def one_device(sub_key):
        key_owner, key_place, key_first, key_second = jax.random.split(sub_key, 4)
        owners = jax.random.permutation(key_owner, N_TOK)
        picked = owners[jnp.arange(BLK_DEV) // CAP]
        picked = picked[jax.random.permutation(key_place, BLK_DEV)]
        first_draw = jax.random.randint(key_first, (BLK_DEV,), 0, ADP_DEV)
        second = jax.random.randint(key_second, (BLK_DEV,), 0, ADP_DEV)
        local_row = jnp.minimum(first_draw, second)
        return inverse[picked * ADP_DEV + local_row]
    return jax.vmap(one_device)(device_keys).astype(jnp.int32)


def level_of(rng, dims, cuts, low, high):
    factor_of, own = 1.0, jax.random.fold_in(rng, 6)
    for position, parts in cuts:
        heights = jnp.exp(jax.random.uniform(jax.random.fold_in(own, position), (parts,), jnp.float32, low / len(cuts), high / len(cuts)))
        factor_of = factor_of * jnp.repeat(heights, dims[position] // parts).reshape([-1 if axis == position else 1 for axis in range(len(dims))])
    return factor_of


def profile(count, total, reach, skew):
    weights = [(1 << 20) // math.isqrt(standing ** skew) + 1 for standing in range(2, count + 1)]
    spare, holding = total - reach - (count - 1), [1] * (count - 1)
    while spare > 0:
        candidates = [i for i in range(count - 1) if holding[i] < reach]
        pool, remaining = sum([weights[i] for i in candidates]), spare
        for i in candidates:
            addition = min(reach - holding[i], max(1, remaining * weights[i] // pool), spare)
            holding[i] = holding[i] + addition
            spare = spare - addition
    return np.array([reach] + holding)


def uneven(own_key, count, total, limit, lean):
    if count == 2:
        one = jax.random.randint(own_key, (), max(1, total - limit), min(limit, total - 1) + 1)
        return jnp.stack([one, total - one])
    tallies = jnp.asarray(profile(count, total, limit, lean), jnp.int32)
    twos = (count - 1) // 2
    donor, sink = tallies[1:1 + 2 * twos:2], tallies[2:2 + 2 * twos:2]
    slack = jnp.minimum(donor - 1, limit - sink)
    moved = jax.random.randint(jax.random.fold_in(own_key, 1), (twos,), 0, 1 << 20) % (slack + 1)
    tallies = tallies.at[1:1 + 2 * twos:2].set(donor - moved).at[2:2 + 2 * twos:2].set(sink + moved)
    return tallies[jax.random.permutation(jax.random.fold_in(own_key, 2), count)]


def noise(own_key, dims, width, bound, cuts=(), kind=jnp.bfloat16):
    factor_of = level_of(own_key, dims, cuts, -0.22, 0.18) if cuts else 1.0
    entries = jax.random.normal(own_key, dims, jnp.float32) * width * factor_of
    return jnp.minimum(jnp.maximum(entries, -bound), bound).astype(kind)


def setup_inputs(seed: int = 0, part: int = 0) -> dict:
    keys = jax.random.split(jax.random.key(seed), 9)
    part_keys = jax.random.split(jax.random.fold_in(keys[8], part), 9)
    inputs = noise(part_keys[0], (TOKENS, D), 1.0, 6.0, ((0, 4), (1, 4)))
    base_weight = noise(keys[1], (D, 2 * KV), D ** -0.5, 0.078125, ((0, 4),))
    panel_a = noise(part_keys[2], (ADAPTERS, R, D), D ** -0.5, 0.078125, ((0, 4), (2, 4)))
    panel_b = noise(part_keys[3], (ADAPTERS, R, 2 * KV), R ** -0.5, 0.75, ((0, 4), (2, 4)))
    teacher = noise(part_keys[4], (TOKENS, 2 * KV), 1.0, 6.0, ((0, 4), (1, 4)))
    block_ids = draw_block_ids(jax.random.fold_in(jax.random.fold_in(keys[8], part), 71), part)
    home_rows = draw_home_rows(jax.random.fold_in(jax.random.fold_in(keys[8], part), 71), part)
    live_blocks = uneven(part_keys[7], N_TOK, N_TOK * BLK_DEV * 3 // 5, BLK_DEV, 1).astype(jnp.int32)
    return dict(inputs=inputs, base_weight=base_weight, panel_a=panel_a, panel_b=panel_b, teacher=teacher, block_ids=block_ids, home_rows=home_rows, live_blocks=live_blocks)


adapter_scale = 2.0


def reference(inputs, base_weight, panel_a, panel_b, teacher, block_ids, home_rows, live_blocks):
    pieces = N_MP * N_SUB
    width_piece = D // pieces

    def piece_sum(total, index):
        first_col = (index * width_piece).astype(jnp.int32)
        cols_in = lax.dynamic_slice_in_dim(inputs, first_col, width_piece, 1)
        rows_w = lax.dynamic_slice_in_dim(base_weight, first_col, width_piece, 0)
        partial_value = jnp.dot(cols_in, rows_w, preferred_element_type=jnp.float32).astype(jnp.bfloat16)
        partial_value = lax.optimization_barrier(partial_value)
        return total + partial_value.astype(jnp.float32), None

    frozen_base_output, _ = lax.scan(piece_sum, jnp.zeros((TOKENS, 2 * KV), jnp.float32), jnp.arange(pieces, dtype=jnp.int32))
    blocks = TOKENS // BLK
    slot_rows = home_rows[block_ids.reshape(-1)].astype(jnp.int32)
    live_mask = (jnp.arange(BLK_DEV)[None, :] < live_blocks[:, None]).reshape(-1).astype(jnp.float32)
    input_blocks = inputs.reshape(blocks, BLK, D)
    base_blocks = frozen_base_output.reshape(blocks, BLK, 2 * KV)
    teacher_blocks = teacher.reshape(blocks, BLK, 2 * KV)

    def per_block(packed):
        row_block, frozen_base_block, teacher_output, slot, active_row_flag = packed
        down_map = panel_a[slot]
        up_weight_matrix = panel_b[slot]
        rank_activations = jnp.dot(down_map, row_block.T, preferred_element_type=jnp.float32).astype(jnp.bfloat16)
        adapter_delta_output = jnp.dot(rank_activations.T, up_weight_matrix, preferred_element_type=jnp.float32)
        student_error = (frozen_base_block + adapter_scale * adapter_delta_output - teacher_output.astype(jnp.float32)) * active_row_flag
        output_gradient_rows = (student_error / BLK).astype(jnp.bfloat16)
        up_weight_gradient = adapter_scale * jnp.dot(rank_activations, output_gradient_rows, preferred_element_type=jnp.float32)
        rank_gradient_rows = (adapter_scale * jnp.dot(up_weight_matrix, output_gradient_rows.T, preferred_element_type=jnp.float32)).astype(jnp.bfloat16)
        grad_down = jnp.dot(rank_gradient_rows, row_block, preferred_element_type=jnp.float32)
        return grad_down, up_weight_gradient

    grad_down, up_weight_gradient = lax.map(per_block, (input_blocks, base_blocks, teacher_blocks, slot_rows, live_mask))
    grad_a = jax.ops.segment_sum(grad_down, slot_rows, num_segments=ADAPTERS).astype(jnp.bfloat16)
    grad_b = jax.ops.segment_sum(up_weight_gradient, slot_rows, num_segments=ADAPTERS).astype(jnp.bfloat16)
    return (grad_a, grad_b)
```

```python
import jax
import jax.numpy as jnp
import functools

from jax import lax
from jax.experimental import pallas as pl
from jax.experimental.pallas import tpu as pltpu
from jax.sharding import PartitionSpec as P

BLK = 128


adapter_scale = 2.0


def padded_exchange(inputs, base_weight, panel_a, panel_b, teacher, block_ids, home_rows, live_blocks):
    width_piece = inputs.shape[1]
    block_count = inputs.shape[0] // BLK
    tok_count = lax.axis_size("tok")
    own_index = lax.axis_index("tok")
    capacity = max(1, 2 * block_count // tok_count)
    slot_total = tok_count * capacity
    adapters_here = panel_a.shape[0]
    rank_width = panel_a.shape[1]
    col_width = panel_b.shape[2]
    slot_all = home_rows[block_ids]
    owner_all = slot_all // adapters_here
    local_all = slot_all % adapters_here
    earlier = jnp.arange(block_count)[None, :] < jnp.arange(block_count)[:, None]
    same_owner = owner_all[:, :, None] == owner_all[:, None, :]
    rank_all = jnp.sum(same_owner & earlier[None], axis=2)
    place_all = owner_all * capacity + rank_all
    owned_here = owner_all == own_index
    owner_table = (
        owned_here[:, :, None, None]
        & (rank_all[:, :, None, None] == jnp.arange(capacity)[None, None, :, None])
        & (local_all[:, :, None, None] == jnp.arange(adapters_here)[None, None, None, :])
    )
    owner_table = (
        jnp.sum(owner_table, axis=1).reshape(slot_total, adapters_here).astype(jnp.float32)
    )
    place_here = lax.dynamic_index_in_dim(place_all, own_index, 0, keepdims=False)
    take_slots = (place_here[:, None] == jnp.arange(slot_total)[None, :]).astype(jnp.float32)
    live_here = lax.dynamic_index_in_dim(live_blocks, own_index, 0, keepdims=False)
    active_row_list = (jnp.arange(block_count) < live_here).astype(jnp.float32)[:, None, None]
    base_rows = lax.psum_scatter(
        lax.dot_general(
            base_weight, inputs, (((0,), (1,)), ((), ())), preferred_element_type=jnp.float32
        ).astype(jnp.bfloat16),
        ("mp", "sub"),
        scatter_dimension=0,
        tiled=True,
    ).astype(jnp.float32)
    frozen_base_output = base_rows.T.reshape(block_count, BLK, col_width)
    teacher_output = teacher.reshape(block_count, BLK, col_width).astype(jnp.float32)
    row_blocks = inputs.reshape(block_count, BLK, width_piece)
    down_flat = panel_a.reshape(adapters_here, rank_width * width_piece)
    up_flat = panel_b.reshape(adapters_here, rank_width * col_width)
    table_low = owner_table.astype(jnp.bfloat16)
    slots_low = take_slots.astype(jnp.bfloat16)
    slot_down = jnp.dot(table_low, down_flat, preferred_element_type=jnp.float32).astype(
        jnp.bfloat16
    )
    slot_up = jnp.dot(table_low, up_flat, preferred_element_type=jnp.float32).astype(jnp.bfloat16)

    def collect(grads):
        summed = jnp.dot(
            owner_table.T,
            grads.reshape(slot_total, -1),
            precision=lax.Precision.HIGHEST,
            preferred_element_type=jnp.float32,
        )
        return summed

    sent_down = slot_down.reshape(tok_count, capacity, -1)
    sent_up = slot_up.reshape(tok_count, capacity, -1)
    got_down, got_up = (
        lax.all_to_all(sent_down, "tok", split_axis=0, concat_axis=0, tiled=True),
        lax.all_to_all(sent_up, "tok", split_axis=0, concat_axis=0, tiled=True),
    )
    block_down = jnp.dot(
        slots_low, got_down.reshape(slot_total, -1), preferred_element_type=jnp.float32
    )
    block_down = block_down.astype(jnp.bfloat16).reshape(block_count, rank_width, width_piece)
    block_up = jnp.dot(
        slots_low, got_up.reshape(slot_total, -1), preferred_element_type=jnp.float32
    )
    block_up = block_up.astype(jnp.bfloat16).reshape(block_count, rank_width, col_width)
    acts_part = jnp.einsum(
        "jrd,jtd->jrt", block_down, row_blocks, preferred_element_type=jnp.float32
    )
    rank_activations = lax.psum(acts_part.astype(jnp.bfloat16), ("mp", "sub"))
    adapter_delta_output = jnp.einsum(
        "jrt,jrc->jtc", rank_activations, block_up, preferred_element_type=jnp.float32
    )
    student_error = (
        frozen_base_output + adapter_scale * adapter_delta_output - teacher_output
    ) * active_row_list
    output_gradient_rows = (student_error / BLK).astype(jnp.bfloat16)
    up_weight_gradient = adapter_scale * jnp.einsum(
        "jrt,jtc->jrc", rank_activations, output_gradient_rows, preferred_element_type=jnp.float32
    )
    partial_gradient_sums = adapter_scale * jnp.einsum(
        "jtc,jrc->jrt", output_gradient_rows, block_up, preferred_element_type=jnp.float32
    )
    rank_gradient_rows = lax.psum(partial_gradient_sums.astype(jnp.bfloat16), ("mp", "sub"))
    grad_down = jnp.einsum(
        "jrt,jtd->jrd", rank_gradient_rows, row_blocks, preferred_element_type=jnp.float32
    )
    back_down = jnp.dot(
        take_slots.T,
        grad_down.reshape(block_count, -1),
        precision=lax.Precision.HIGHEST,
        preferred_element_type=jnp.float32,
    ).reshape(tok_count, capacity, -1)
    back_up = jnp.dot(
        take_slots.T,
        up_weight_gradient.reshape(block_count, -1),
        precision=lax.Precision.HIGHEST,
        preferred_element_type=jnp.float32,
    ).reshape(tok_count, capacity, -1)
    held_down, held_up = (
        lax.all_to_all(
            back_down.astype(jnp.bfloat16), "tok", split_axis=0, concat_axis=0, tiled=True
        ).astype(back_down.dtype),
        lax.all_to_all(
            back_up.astype(jnp.bfloat16), "tok", split_axis=0, concat_axis=0, tiled=True
        ).astype(back_up.dtype),
    )
    grad_a = collect(held_down)
    grad_b = collect(held_up)
    grad_a = grad_a.reshape(adapters_here, rank_width, width_piece).astype(jnp.bfloat16)
    grad_b = grad_b.reshape(adapters_here, rank_width, col_width).astype(jnp.bfloat16)
    return (grad_a, grad_b)


STEPS = (6, 8, 10, 12, 14, 16, 20)
SKEW = 2
MIB = 1024 * 1024
VMEM_LIMIT = 56 * MIB


def table_layout(places, block_count, adapters_here):
    sizes = dict(
        out_right=places,
        out_left=places,
        back_right=places,
        back_left=places,
        kind=block_count,
        source=block_count,
        head=adapters_here,
        chain=block_count + 2 * places,
        count=1,
    )
    at, offset = {}, 0
    for name, size in sizes.items():
        at[name] = offset
        offset += size
    return at, offset


def table_kernel(tok_count, block_count, adapters_here, places, ids, home, live, table, slot, free, items):
    at, total = table_layout(places, block_count, adapters_here)
    me = lax.axis_index("tok")

    def clear(i, carry):
        table[i] = jnp.int32(-1)
        return carry

    lax.fori_loop(0, total, clear, 0)

    def look_up(i, carry):
        t, j = lax.div(i, block_count), lax.rem(i, block_count)
        slot[i] = jnp.where(j < live[t], home[ids[t, j]], -1)
        return carry

    lax.fori_loop(0, tok_count * block_count, look_up, 0)

    def own(j, carry):
        table[at["kind"] + j] = jnp.int32(0)
        table[at["source"] + j] = jnp.int32(0)
        row = slot[me * block_count + j]
        local = row - me * adapters_here

        @pl.when((row >= 0) & (local >= 0) & (local < adapters_here))
        def _():
            table[at["source"] + j] = local
            table[at["chain"] + j] = table[at["head"] + local]
            table[at["head"] + local] = j

        return carry

    lax.fori_loop(0, block_count, own, 0)

    used = jnp.int32(0)
    for right in (True, False):

        def reset(p, carry):
            free[p] = jnp.int32(0 if right else tok_count - 1)
            return carry

        lax.fori_loop(0, places, reset, 0)
        owners = range(tok_count - 1) if right else range(tok_count - 1, 0, -1)
        for s in owners:
            first, last = (s + 1, tok_count) if right else (0, s)

            def gather(i, n):
                row = slot[i]
                hit = (row >= s * adapters_here) & (row < (s + 1) * adapters_here)

                @pl.when(hit)
                def _():
                    items[n] = i

                return n + hit.astype(jnp.int32)

            n = lax.fori_loop(first * block_count, last * block_count, gather, jnp.int32(0))

            def assign(p, carry):
                k, most = carry
                ok = (free[p] <= s) if right else (free[p] >= s)
                ok = ok & (k < n)

                @pl.when(ok)
                def _():
                    i = items[k]
                    d, j = lax.div(i, block_count), lax.rem(i, block_count)
                    local = slot[i] - s * adapters_here
                    free[p] = d

                    @pl.when(me == s)
                    def _():
                        table[at["out_right" if right else "out_left"] + p] = local
                        item = block_count + p + (places if right else 0)
                        table[at["chain"] + item] = table[at["head"] + local]
                        table[at["head"] + local] = item

                    @pl.when(me == d)
                    def _():
                        table[at["kind"] + j] = jnp.int32(1 if right else 2)
                        table[at["source"] + j] = p
                        table[at["back_left" if right else "back_right"] + p] = j

                return (k + ok.astype(jnp.int32), jnp.where(ok, jnp.maximum(most, p + 1), most))

            _, used = lax.fori_loop(0, places, assign, (jnp.int32(0), used))
    table[at["count"]] = used


def make_table(block_ids, home_rows, live_blocks, adapters_here, places):
    tok_count, block_count = block_ids.shape
    _, total = table_layout(places, block_count, adapters_here)
    smem = pl.BlockSpec(memory_space=pltpu.SMEM)
    return pl.pallas_call(
        functools.partial(table_kernel, tok_count, block_count, adapters_here, places),
        out_shape=jax.ShapeDtypeStruct((total,), jnp.int32),
        in_specs=[smem] * 3,
        out_specs=smem,
        scratch_shapes=[
            pltpu.SMEM((tok_count * block_count,), jnp.int32),
            pltpu.SMEM((places,), jnp.int32),
            pltpu.SMEM((tok_count * block_count,), jnp.int32),
        ],
        name="place_table",
    )(block_ids, home_rows, live_blocks)


def run_belts(
    tok_count, steps, at_right, at_left, table, wide, narrow,
    from_left, from_right, to_right, to_left, send_sem, recv_sem,
):
    me = lax.axis_index("tok")
    split = wide.shape[2]
    barrier = pltpu.get_barrier_semaphore()

    @pl.when(me > 0)
    def _():
        pl.semaphore_signal(barrier, inc=1, device_id={"tok": me - 1})

    @pl.when(me < tok_count - 1)
    def _():
        pl.semaphore_signal(barrier, inc=1, device_id={"tok": me + 1})

    @pl.when((me == 0) | (me == tok_count - 1))
    def _():
        pl.semaphore_wait(barrier, 1)

    @pl.when((me > 0) & (me < tok_count - 1))
    def _():
        pl.semaphore_wait(barrier, 2)

    def copy(belt, p, target):
        outgoing, incoming = (to_right, from_left) if belt == 0 else (to_left, from_right)
        return pltpu.make_async_remote_copy(
            src_ref=outgoing.at[p],
            dst_ref=incoming.at[p],
            send_sem=send_sem.at[belt, p],
            recv_sem=recv_sem.at[belt, p],
            device_id={"tok": target},
        )

    def belt_step(belt, p):
        position = me if belt == 0 else tok_count - 1 - me
        target = me + 1 if belt == 0 else me - 1
        outgoing, incoming = (to_right, from_left) if belt == 0 else (to_left, from_right)
        at = at_right if belt == 0 else at_left
        inside = (p >= 0) & (p < steps)

        @pl.when(inside & (position > 0))
        def _():
            copy(belt, p, target).wait_recv()

        @pl.when(inside & (position == 0))
        def _():
            own = jnp.maximum(table[at + p], 0)
            outgoing[p, :, :split] = wide[own]
            outgoing[p, :, split:] = narrow[own]

        @pl.when(inside & (position > 0) & (position < tok_count - 1))
        def _():
            own = table[at + p]
            fresh = own >= 0
            own = jnp.maximum(own, 0)
            outgoing[p, :, :split] = jnp.where(fresh, wide[own], incoming[p, :, :split])
            outgoing[p, :, split:] = jnp.where(fresh, narrow[own], incoming[p, :, split:])

        @pl.when(inside & (position < tok_count - 1))
        def _():
            copy(belt, p, target).start()

    def one_round(r, carry):
        belt_step(0, r - SKEW * me)
        belt_step(1, r - SKEW * (tok_count - 1 - me))
        return carry

    lax.fori_loop(0, steps + SKEW * (tok_count - 1), one_round, 0)

    def finish(p, carry):
        @pl.when(me < tok_count - 1)
        def _():
            copy(0, p, me + 1).wait_send()

        @pl.when(me > 0)
        def _():
            copy(1, p, me - 1).wait_send()

        return carry

    lax.fori_loop(0, steps, finish, 0)


def out_kernel(
    tok_count, steps, at, table, panel_a, panel_b, down, up,
    from_left, from_right, to_right, to_left, send_sem, recv_sem,
):
    run_belts(
        tok_count, steps, at["out_right"], at["out_left"], table, panel_a, panel_b,
        from_left, from_right, to_right, to_left, send_sem, recv_sem,
    )
    split = panel_a.shape[2]

    def pick(j, carry):
        kind, source = table[at["kind"] + j], table[at["source"] + j]
        own = jnp.where(kind == 0, source, 0)
        left = jnp.where(kind == 1, source, 0)
        right = jnp.where(kind == 2, source, 0)
        down[j] = jnp.where(
            kind == 0,
            panel_a[own],
            jnp.where(kind == 1, from_left[left, :, :split], from_right[right, :, :split]),
        )
        up[j] = jnp.where(
            kind == 0,
            panel_b[own],
            jnp.where(kind == 1, from_left[left, :, split:], from_right[right, :, split:]),
        )
        return carry

    lax.fori_loop(0, down.shape[0], pick, 0)


def fetch(steps, order, tok_count, at, table, panel_a, panel_b, block_count):
    rank, wide = panel_a.shape[1:]
    narrow = panel_b.shape[2]
    vmem = pl.BlockSpec(memory_space=pltpu.VMEM)
    slots = pltpu.VMEM((steps, rank, wide + narrow), jnp.bfloat16)
    return pl.pallas_call(
        functools.partial(out_kernel, tok_count, steps, at),
        out_shape=(
            jax.ShapeDtypeStruct((block_count, rank, wide), jnp.bfloat16),
            jax.ShapeDtypeStruct((block_count, rank, narrow), jnp.bfloat16),
        ),
        in_specs=[pl.BlockSpec(memory_space=pltpu.SMEM), vmem, vmem],
        out_specs=(vmem, vmem),
        scratch_shapes=[slots] * 4
        + [pltpu.SemaphoreType.DMA((2, steps)), pltpu.SemaphoreType.DMA((2, steps))],
        compiler_params=pltpu.CompilerParams(
            collective_id=order, has_side_effects=True, vmem_limit_bytes=VMEM_LIMIT
        ),
        name="fetch_panels",
    )(table, panel_a, panel_b)


def back_kernel(
    tok_count, steps, at, table, grad_down, grad_up, from_left, from_right,
    to_right, to_left, send_sem, recv_sem,
):
    run_belts(
        tok_count, steps, at["back_right"], at["back_left"], table, grad_down, grad_up,
        from_left, from_right, to_right, to_left, send_sem, recv_sem,
    )


def sum_kernel(
    at, places, block_count, table, grad_down, grad_up, from_left, from_right, grad_a, grad_b
):
    split = grad_down.shape[2]
    row = pl.program_id(0)

    head = table[at["head"] + row]

    def more(state):
        return state[0] >= 0

    def step(state):
        item, sum_a, sum_b = state
        belt = item - block_count
        own = jnp.where(belt < 0, item, 0)
        left = jnp.where((belt >= 0) & (belt < places), belt, 0)
        right = jnp.where(belt >= places, belt - places, 0)
        term_a = jnp.where(
            belt < 0,
            grad_down[own],
            jnp.where(belt < places, from_left[left, :, :split], from_right[right, :, :split]),
        )
        term_b = jnp.where(
            belt < 0,
            grad_up[own],
            jnp.where(belt < places, from_left[left, :, split:], from_right[right, :, split:]),
        )
        return (
            table[at["chain"] + item],
            sum_a + term_a.astype(jnp.float32),
            sum_b + term_b.astype(jnp.float32),
        )

    _, sum_a, sum_b = lax.while_loop(
        more,
        step,
        (head, jnp.zeros(grad_a.shape[1:], jnp.float32), jnp.zeros(grad_b.shape[1:], jnp.float32)),
    )
    grad_a[0] = sum_a.astype(jnp.bfloat16)
    grad_b[0] = sum_b.astype(jnp.bfloat16)


def give_back(steps, order, tok_count, at, places, adapters_here, table, grad_down, grad_up):
    block_count, rank, wide = grad_down.shape
    narrow = grad_up.shape[2]
    vmem = pl.BlockSpec(memory_space=pltpu.VMEM)
    smem = pl.BlockSpec(memory_space=pltpu.SMEM)
    slots = (steps, rank, wide + narrow)
    from_left, from_right = pl.pallas_call(
        functools.partial(back_kernel, tok_count, steps, at),
        out_shape=(jax.ShapeDtypeStruct(slots, jnp.bfloat16),) * 2,
        in_specs=[smem, vmem, vmem],
        out_specs=(vmem, vmem),
        scratch_shapes=[pltpu.VMEM(slots, jnp.bfloat16)] * 2
        + [pltpu.SemaphoreType.DMA((2, steps)), pltpu.SemaphoreType.DMA((2, steps))],
        compiler_params=pltpu.CompilerParams(
            collective_id=order, has_side_effects=True, vmem_limit_bytes=VMEM_LIMIT
        ),
        name="return_grads",
    )(table, grad_down, grad_up)
    return pl.pallas_call(
        functools.partial(sum_kernel, at, places, block_count),
        grid=(adapters_here,),
        out_shape=(
            jax.ShapeDtypeStruct((adapters_here, rank, wide), jnp.bfloat16),
            jax.ShapeDtypeStruct((adapters_here, rank, narrow), jnp.bfloat16),
        ),
        in_specs=[smem, vmem, vmem, vmem, vmem],
        out_specs=(
            pl.BlockSpec((1, rank, wide), lambda i: (i, 0, 0)),
            pl.BlockSpec((1, rank, narrow), lambda i: (i, 0, 0)),
        ),
        compiler_params=pltpu.CompilerParams(vmem_limit_bytes=VMEM_LIMIT),
        name="sum_grads",
    )(table, grad_down, grad_up, from_left, from_right)


def on_device(inputs, base_weight, panel_a, panel_b, teacher, block_ids, home_rows, live_blocks):
    width_piece = inputs.shape[1]
    block_count = inputs.shape[0] // BLK
    tok_count = lax.axis_size("tok")
    capacity = max(1, 2 * block_count // tok_count)
    adapters_here, rank_width, _ = panel_a.shape
    col_width = panel_b.shape[2]
    places = capacity * (tok_count // 2) * (tok_count - tok_count // 2)
    slot_bytes = 2 * rank_width * (width_piece + col_width)
    if 4 * places * slot_bytes > 24 * MIB:
        return padded_exchange(
            inputs, base_weight, panel_a, panel_b, teacher, block_ids, home_rows, live_blocks
        )
    own_index = lax.axis_index("tok")
    at, _ = table_layout(places, block_count, adapters_here)
    table = make_table(block_ids, home_rows, live_blocks, adapters_here, places)
    needed = table[at["count"]:at["count"] + 1]
    groups = lax.axis_size("groups")
    most = needed
    for shift in range(1, groups):
        other = lax.ppermute(needed, "groups", [(g, (g + shift) % groups) for g in range(groups)])
        most = jnp.maximum(most, other)
    steps_list = [s for s in STEPS if s < places] + [places]
    branch = jnp.sum(most[0] > jnp.array(steps_list[:-1], jnp.int32)).astype(jnp.int32)

    base_rows = lax.psum_scatter(
        lax.dot_general(
            base_weight, inputs, (((0,), (1,)), ((), ())), preferred_element_type=jnp.float32
        ).astype(jnp.bfloat16),
        ("mp", "sub"),
        scatter_dimension=0,
        tiled=True,
    ).astype(jnp.float32)
    frozen_base_output = base_rows.T.reshape(block_count, BLK, col_width)
    teacher_output = teacher.reshape(block_count, BLK, col_width).astype(jnp.float32)
    row_blocks = inputs.reshape(block_count, BLK, width_piece)
    live_here = lax.dynamic_index_in_dim(live_blocks, own_index, 0, keepdims=False)
    active_row_list = (jnp.arange(block_count) < live_here).astype(jnp.float32)[:, None, None]

    block_down, block_up = lax.switch(
        branch,
        [
            functools.partial(
                lambda steps, order, t, a, b: fetch(
                    steps, order, tok_count, at, t, a, b, block_count
                ),
                steps,
                order,
            )
            for order, steps in enumerate(steps_list)
        ],
        table,
        panel_a,
        panel_b,
    )
    acts_part = jnp.einsum(
        "jrd,jtd->jrt", block_down, row_blocks, preferred_element_type=jnp.float32
    )
    rank_activations = lax.psum(acts_part.astype(jnp.bfloat16), ("mp", "sub"))
    adapter_delta_output = jnp.einsum(
        "jrt,jrc->jtc", rank_activations, block_up, preferred_element_type=jnp.float32
    )
    student_error = (
        frozen_base_output + adapter_scale * adapter_delta_output - teacher_output
    ) * active_row_list
    output_gradient_rows = (student_error / BLK).astype(jnp.bfloat16)
    up_weight_gradient = adapter_scale * jnp.einsum(
        "jrt,jtc->jrc", rank_activations, output_gradient_rows, preferred_element_type=jnp.float32
    )
    partial_gradient_sums = adapter_scale * jnp.einsum(
        "jtc,jrc->jrt", output_gradient_rows, block_up, preferred_element_type=jnp.float32
    )
    rank_gradient_rows = lax.psum(partial_gradient_sums.astype(jnp.bfloat16), ("mp", "sub"))
    grad_down = jnp.einsum(
        "jrt,jtd->jrd", rank_gradient_rows, row_blocks, preferred_element_type=jnp.float32
    )
    return lax.switch(
        branch,
        [
            functools.partial(
                lambda steps, order, t, a, b: give_back(
                    steps, order, tok_count, at, places, adapters_here, t, a, b
                ),
                steps,
                len(steps_list) + order,
            )
            for order, steps in enumerate(steps_list)
        ],
        table,
        grad_down.astype(jnp.bfloat16),
        up_weight_gradient.astype(jnp.bfloat16),
    )


def solution(mesh):
    placed = (
        P(("groups", "tok"), ("mp", "sub")),
        P(("mp", "sub"), None),
        P(("groups", "tok"), None, ("mp", "sub")),
        P(("groups", "tok"), None, ("mp", "sub")),
        P(("groups", "tok"), ("mp", "sub")),
        P("groups", None),
        P("groups"),
        P("groups"),
    )
    return jax.shard_map(
        on_device,
        mesh=mesh,
        in_specs=placed,
        out_specs=(
            P(("groups", "tok"), None, ("mp", "sub")),
            P(("groups", "tok"), None, ("mp", "sub")),
        ),
        check_vma=False,
    )
```

```python
import jax
import jax.numpy as jnp
import functools
import math

from jax import lax
from jax.experimental import pallas as pl
from jax.experimental.pallas import tpu as pltpu
from jax.sharding import PartitionSpec as P

BLK = 128


adapter_scale = 2.0


def padded_exchange(inputs, base_weight, panel_a, panel_b, teacher, block_ids, home_rows, live_blocks):
    width_piece = inputs.shape[1]
    block_count = inputs.shape[0] // BLK
    tok_count = lax.axis_size("tok")
    own_index = lax.axis_index("tok")
    capacity = max(1, 2 * block_count // tok_count)
    slot_total = tok_count * capacity
    adapters_here = panel_a.shape[0]
    rank_width = panel_a.shape[1]
    col_width = panel_b.shape[2]
    slot_all = home_rows[block_ids]
    owner_all = slot_all // adapters_here
    local_all = slot_all % adapters_here
    earlier = jnp.arange(block_count)[None, :] < jnp.arange(block_count)[:, None]
    same_owner = owner_all[:, :, None] == owner_all[:, None, :]
    rank_all = jnp.sum(same_owner & earlier[None], axis=2)
    place_all = owner_all * capacity + rank_all
    owned_here = owner_all == own_index
    owner_table = (
        owned_here[:, :, None, None]
        & (rank_all[:, :, None, None] == jnp.arange(capacity)[None, None, :, None])
        & (local_all[:, :, None, None] == jnp.arange(adapters_here)[None, None, None, :])
    )
    owner_table = (
        jnp.sum(owner_table, axis=1).reshape(slot_total, adapters_here).astype(jnp.float32)
    )
    place_here = lax.dynamic_index_in_dim(place_all, own_index, 0, keepdims=False)
    take_slots = (place_here[:, None] == jnp.arange(slot_total)[None, :]).astype(jnp.float32)
    live_here = lax.dynamic_index_in_dim(live_blocks, own_index, 0, keepdims=False)
    active_row_list = (jnp.arange(block_count) < live_here).astype(jnp.float32)[:, None, None]
    base_rows = lax.psum_scatter(
        lax.dot_general(
            base_weight, inputs, (((0,), (1,)), ((), ())), preferred_element_type=jnp.float32
        ).astype(jnp.bfloat16),
        ("mp", "sub"),
        scatter_dimension=0,
        tiled=True,
    ).astype(jnp.float32)
    frozen_base_output = base_rows.T.reshape(block_count, BLK, col_width)
    teacher_output = teacher.reshape(block_count, BLK, col_width).astype(jnp.float32)
    row_blocks = inputs.reshape(block_count, BLK, width_piece)
    down_flat = panel_a.reshape(adapters_here, rank_width * width_piece)
    up_flat = panel_b.reshape(adapters_here, rank_width * col_width)
    table_low = owner_table.astype(jnp.bfloat16)
    slots_low = take_slots.astype(jnp.bfloat16)
    slot_down = jnp.dot(table_low, down_flat, preferred_element_type=jnp.float32).astype(
        jnp.bfloat16
    )
    slot_up = jnp.dot(table_low, up_flat, preferred_element_type=jnp.float32).astype(jnp.bfloat16)

    def collect(grads):
        summed = jnp.dot(
            owner_table.T,
            grads.reshape(slot_total, -1),
            precision=lax.Precision.HIGHEST,
            preferred_element_type=jnp.float32,
        )
        return summed

    sent_down = slot_down.reshape(tok_count, capacity, -1)
    sent_up = slot_up.reshape(tok_count, capacity, -1)
    got_down, got_up = (
        lax.all_to_all(sent_down, "tok", split_axis=0, concat_axis=0, tiled=True),
        lax.all_to_all(sent_up, "tok", split_axis=0, concat_axis=0, tiled=True),
    )
    block_down = jnp.dot(
        slots_low, got_down.reshape(slot_total, -1), preferred_element_type=jnp.float32
    )
    block_down = block_down.astype(jnp.bfloat16).reshape(block_count, rank_width, width_piece)
    block_up = jnp.dot(
        slots_low, got_up.reshape(slot_total, -1), preferred_element_type=jnp.float32
    )
    block_up = block_up.astype(jnp.bfloat16).reshape(block_count, rank_width, col_width)
    acts_part = jnp.einsum(
        "jrd,jtd->jrt", block_down, row_blocks, preferred_element_type=jnp.float32
    )
    rank_activations = lax.psum(acts_part.astype(jnp.bfloat16), ("mp", "sub"))
    adapter_delta_output = jnp.einsum(
        "jrt,jrc->jtc", rank_activations, block_up, preferred_element_type=jnp.float32
    )
    student_error = (
        frozen_base_output + adapter_scale * adapter_delta_output - teacher_output
    ) * active_row_list
    output_gradient_rows = (student_error / BLK).astype(jnp.bfloat16)
    up_weight_gradient = adapter_scale * jnp.einsum(
        "jrt,jtc->jrc", rank_activations, output_gradient_rows, preferred_element_type=jnp.float32
    )
    partial_gradient_sums = adapter_scale * jnp.einsum(
        "jtc,jrc->jrt", output_gradient_rows, block_up, preferred_element_type=jnp.float32
    )
    rank_gradient_rows = lax.psum(partial_gradient_sums.astype(jnp.bfloat16), ("mp", "sub"))
    grad_down = jnp.einsum(
        "jrt,jtd->jrd", rank_gradient_rows, row_blocks, preferred_element_type=jnp.float32
    )
    back_down = jnp.dot(
        take_slots.T,
        grad_down.reshape(block_count, -1),
        precision=lax.Precision.HIGHEST,
        preferred_element_type=jnp.float32,
    ).reshape(tok_count, capacity, -1)
    back_up = jnp.dot(
        take_slots.T,
        up_weight_gradient.reshape(block_count, -1),
        precision=lax.Precision.HIGHEST,
        preferred_element_type=jnp.float32,
    ).reshape(tok_count, capacity, -1)
    held_down, held_up = (
        lax.all_to_all(
            back_down.astype(jnp.bfloat16), "tok", split_axis=0, concat_axis=0, tiled=True
        ).astype(back_down.dtype),
        lax.all_to_all(
            back_up.astype(jnp.bfloat16), "tok", split_axis=0, concat_axis=0, tiled=True
        ).astype(back_up.dtype),
    )
    grad_a = collect(held_down)
    grad_b = collect(held_up)
    grad_a = grad_a.reshape(adapters_here, rank_width, width_piece).astype(jnp.bfloat16)
    grad_b = grad_b.reshape(adapters_here, rank_width, col_width).astype(jnp.bfloat16)
    return (grad_a, grad_b)


STEPS = (7, 8, 9, 10, 11, 12, 13, 14, 16, 20)
SKEW = 4
CUTS = 2
MIB = 1024 * 1024
VMEM_LIMIT = 56 * MIB


def table_layout(places, block_count, adapters_here):
    sizes = dict(
        out_right=places,
        out_left=places,
        back_right=places,
        back_left=places,
        kind=block_count,
        source=block_count,
        head=adapters_here,
        chain=block_count + 2 * places,
        again=block_count,
        live=1,
        count=1,
    )
    at, offset = {}, 0
    for name, size in sizes.items():
        at[name] = offset
        offset += size
    return at, offset


def table_kernel(tok_count, block_count, adapters_here, places, ids, home, live, table, slot, free, items, seen, first_of
):
    at, total = table_layout(places, block_count, adapters_here)
    me = lax.axis_index("tok")

    def clear(i, carry):
        table[i] = jnp.int32(-1)
        return carry

    lax.fori_loop(0, total, clear, 0, unroll=8)

    def forget(i, carry):
        seen[i] = jnp.int32(-1)
        return carry

    lax.fori_loop(0, tok_count * adapters_here, forget, 0, unroll=8)
    table[at["live"]] = live[me]

    def look_up(i, carry):
        t, j = lax.div(i, block_count), lax.rem(i, block_count)
        row = home[ids[t, j]]
        alive = j < live[t]
        before = seen[row]
        twin = alive & (before >= t * block_count)
        slot[i] = jnp.where(alive & jnp.logical_not(twin), row, -1)
        first_of[i] = jnp.where(twin, first_of[jnp.maximum(before, 0)], i)

        @pl.when(alive)
        def _():
            seen[row] = i

        @pl.when(twin & (t == me))
        def _():
            table[at["again"] + lax.rem(before, block_count)] = j

        return carry

    lax.fori_loop(0, tok_count * block_count, look_up, 0)

    def own(j, carry):
        table[at["kind"] + j] = jnp.int32(0)
        table[at["source"] + j] = jnp.int32(0)
        row = slot[me * block_count + j]
        local = row - me * adapters_here

        @pl.when((row >= 0) & (local >= 0) & (local < adapters_here))
        def _():
            table[at["source"] + j] = local
            table[at["chain"] + j] = table[at["head"] + local]
            table[at["head"] + local] = j

        return carry

    lax.fori_loop(0, block_count, own, 0)

    used = jnp.int32(0)
    for right in (True, False):

        def reset(p, carry):
            free[p] = jnp.int32(0 if right else tok_count - 1)
            return carry

        lax.fori_loop(0, places, reset, 0)
        owners = range(tok_count - 1) if right else range(tok_count - 1, 0, -1)
        for s in owners:
            first, last = (s + 1, tok_count) if right else (0, s)

            def gather(i, n):
                row = slot[i]
                hit = (row >= s * adapters_here) & (row < (s + 1) * adapters_here)

                @pl.when(hit)
                def _():
                    items[n] = i

                return n + hit.astype(jnp.int32)

            n = lax.fori_loop(first * block_count, last * block_count, gather, jnp.int32(0))

            def assign(p, carry):
                k, most = carry
                ok = (free[p] <= s) if right else (free[p] >= s)
                ok = ok & (k < n)

                @pl.when(ok)
                def _():
                    i = items[k]
                    d, j = lax.div(i, block_count), lax.rem(i, block_count)
                    local = slot[i] - s * adapters_here
                    free[p] = d

                    @pl.when(me == s)
                    def _():
                        table[at["out_right" if right else "out_left"] + p] = local
                        item = block_count + p + (places if right else 0)
                        table[at["chain"] + item] = table[at["head"] + local]
                        table[at["head"] + local] = item

                    @pl.when(me == d)
                    def _():
                        table[at["kind"] + j] = jnp.int32(1 if right else 2)
                        table[at["source"] + j] = p
                        table[at["back_left" if right else "back_right"] + p] = j

                return (k + ok.astype(jnp.int32), jnp.where(ok, jnp.maximum(most, p + 1), most))

            _, used = lax.fori_loop(0, places, assign, (jnp.int32(0), used))
    table[at["count"]] = used

    def share(j, carry):
        first = lax.rem(first_of[me * block_count + j], block_count)
        table[at["kind"] + j] = table[at["kind"] + first]
        table[at["source"] + j] = table[at["source"] + first]
        return carry

    lax.fori_loop(0, block_count, share, 0)


def make_table(block_ids, home_rows, live_blocks, adapters_here, places):
    tok_count, block_count = block_ids.shape
    _, total = table_layout(places, block_count, adapters_here)
    smem = pl.BlockSpec(memory_space=pltpu.SMEM)
    return pl.pallas_call(
        functools.partial(table_kernel, tok_count, block_count, adapters_here, places),
        out_shape=jax.ShapeDtypeStruct((total,), jnp.int32),
        in_specs=[smem] * 3,
        out_specs=smem,
        scratch_shapes=[
            pltpu.SMEM((tok_count * block_count,), jnp.int32),
            pltpu.SMEM((places,), jnp.int32),
            pltpu.SMEM((tok_count * block_count,), jnp.int32),
            pltpu.SMEM((tok_count * adapters_here,), jnp.int32),
            pltpu.SMEM((tok_count * block_count,), jnp.int32),
        ],
        name="place_table",
    )(block_ids, home_rows, live_blocks)


def run_belts(
    tok_count, steps, at_right, at_left, table, wide, narrow,
    from_left, from_right, to_right, to_left, send_sem, recv_sem,
):
    me = lax.axis_index("tok")
    split = wide.shape[2]
    barrier = pltpu.get_barrier_semaphore()

    @pl.when(me > 0)
    def _():
        pl.semaphore_signal(barrier, inc=1, device_id={"tok": me - 1})

    @pl.when(me < tok_count - 1)
    def _():
        pl.semaphore_signal(barrier, inc=1, device_id={"tok": me + 1})

    @pl.when((me == 0) | (me == tok_count - 1))
    def _():
        pl.semaphore_wait(barrier, 1)

    @pl.when((me > 0) & (me < tok_count - 1))
    def _():
        pl.semaphore_wait(barrier, 2)

    def copy(belt, p, target):
        outgoing, incoming = (to_right, from_left) if belt == 0 else (to_left, from_right)
        return pltpu.make_async_remote_copy(
            src_ref=outgoing.at[p],
            dst_ref=incoming.at[p],
            send_sem=send_sem.at[belt, p],
            recv_sem=recv_sem.at[belt, p],
            device_id={"tok": target},
        )

    def belt_step(belt, p):
        position = me if belt == 0 else tok_count - 1 - me
        target = me + 1 if belt == 0 else me - 1
        outgoing, incoming = (to_right, from_left) if belt == 0 else (to_left, from_right)
        at = at_right if belt == 0 else at_left
        inside = (p >= 0) & (p < steps * CUTS)

        @pl.when(inside & (position > 0))
        def _():
            copy(belt, p, target).wait_recv()

        @pl.when(inside & (position == 0))
        def _():
            own = jnp.maximum(table[at + lax.div(p, CUTS)], 0) * CUTS + lax.rem(p, CUTS)
            outgoing[p, :, :split] = wide[own]
            outgoing[p, :, split:] = narrow[own]

        @pl.when(inside & (position > 0) & (position < tok_count - 1))
        def _():
            own = table[at + lax.div(p, CUTS)]
            fresh = own >= 0
            own = jnp.maximum(own, 0) * CUTS + lax.rem(p, CUTS)
            outgoing[p, :, :split] = jnp.where(fresh, wide[own], incoming[p, :, :split])
            outgoing[p, :, split:] = jnp.where(fresh, narrow[own], incoming[p, :, split:])

        @pl.when(inside & (position < tok_count - 1))
        def _():
            copy(belt, p, target).start()

    def one_round(r, carry):
        belt_step(0, r - SKEW * me)
        belt_step(1, r - SKEW * (tok_count - 1 - me))
        return carry

    lax.fori_loop(0, steps * CUTS + SKEW * (tok_count - 1), one_round, 0)

    def finish(p, carry):
        @pl.when(me < tok_count - 1)
        def _():
            copy(0, p, me + 1).wait_send()

        @pl.when(me > 0)
        def _():
            copy(1, p, me - 1).wait_send()

        return carry

    lax.fori_loop(0, steps * CUTS, finish, 0)


def out_kernel(
    tok_count, steps, at, table, panel_a, panel_b, down, up,
    from_left, from_right, to_right, to_left, send_sem, recv_sem,
):
    run_belts(
        tok_count, steps, at["out_right"], at["out_left"], table, panel_a, panel_b,
        from_left, from_right, to_right, to_left, send_sem, recv_sem,
    )
    split = panel_a.shape[2]

    def pick(j, carry):
        block, cut = lax.div(j, CUTS), lax.rem(j, CUTS)
        kind = table[at["kind"] + block]
        source = table[at["source"] + block] * CUTS + cut
        own = jnp.where(kind == 0, source, 0)
        left = jnp.where(kind == 1, source, 0)
        right = jnp.where(kind == 2, source, 0)
        down[j] = jnp.where(
            kind == 0,
            panel_a[own],
            jnp.where(kind == 1, from_left[left, :, :split], from_right[right, :, :split]),
        )
        up[j] = jnp.where(
            kind == 0,
            panel_b[own],
            jnp.where(kind == 1, from_left[left, :, split:], from_right[right, :, split:]),
        )
        return carry

    lax.fori_loop(0, down.shape[0], pick, 0)


def fetch(steps, order, tok_count, at, table, panel_a, panel_b, block_count):
    rank, wide = panel_a.shape[1:]
    narrow = panel_b.shape[2]
    vmem = pl.BlockSpec(memory_space=pltpu.VMEM)
    slots = pltpu.VMEM((steps * CUTS, rank // CUTS, wide + narrow), jnp.bfloat16)
    down, up = pl.pallas_call(
        functools.partial(out_kernel, tok_count, steps, at),
        out_shape=(
            jax.ShapeDtypeStruct((block_count * CUTS, rank // CUTS, wide), jnp.bfloat16),
            jax.ShapeDtypeStruct((block_count * CUTS, rank // CUTS, narrow), jnp.bfloat16),
        ),
        in_specs=[pl.BlockSpec(memory_space=pltpu.SMEM), vmem, vmem],
        out_specs=(vmem, vmem),
        scratch_shapes=[slots] * 4
        + [pltpu.SemaphoreType.DMA((2, steps * CUTS))] * 2,
        compiler_params=pltpu.CompilerParams(
            collective_id=order, has_side_effects=True, vmem_limit_bytes=VMEM_LIMIT
        ),
        name="fetch_panels",
    )(table, panel_a.reshape(-1, rank // CUTS, wide), panel_b.reshape(-1, rank // CUTS, narrow))
    return down.reshape(block_count, rank, wide), up.reshape(block_count, rank, narrow)


def back_kernel(
    tok_count, steps, at, table, grad_down, grad_up, from_left, from_right,
    to_right, to_left, send_sem, recv_sem,
):
    run_belts(
        tok_count, steps, at["back_right"], at["back_left"], table, grad_down, grad_up,
        from_left, from_right, to_right, to_left, send_sem, recv_sem,
    )


def sum_kernel(
    at, places, block_count, table, grad_down, grad_up, from_left, from_right, grad_a, grad_b,
    sum_a, sum_b,
):
    split = grad_down.shape[2]
    rows = grad_a.shape[0]
    first = pl.program_id(0) * rows

    def one_row(i, carry):
        head = table[at["head"] + first + i]

        @pl.when(head < 0)
        def _():
            grad_a[i] = jnp.zeros(grad_a.shape[1:], jnp.bfloat16)
            grad_b[i] = jnp.zeros(grad_b.shape[1:], jnp.bfloat16)

        @pl.when(head >= 0)
        def _():
            sum_a[...] = jnp.zeros_like(sum_a)
            sum_b[...] = jnp.zeros_like(sum_b)

            def step(item):
                belt = item - block_count

                @pl.when(belt < 0)
                def _():
                    sum_a[...] += grad_down[item].astype(jnp.float32)
                    sum_b[...] += grad_up[item].astype(jnp.float32)

                @pl.when((belt >= 0) & (belt < places))
                def _():
                    sum_a[...] += from_left[belt, :, :split].astype(jnp.float32)
                    sum_b[...] += from_left[belt, :, split:].astype(jnp.float32)

                @pl.when(belt >= places)
                def _():
                    sum_a[...] += from_right[belt - places, :, :split].astype(jnp.float32)
                    sum_b[...] += from_right[belt - places, :, split:].astype(jnp.float32)

                return table[at["chain"] + item]

            lax.while_loop(lambda item: item >= 0, step, head)
            grad_a[i] = sum_a[...].astype(jnp.bfloat16)
            grad_b[i] = sum_b[...].astype(jnp.bfloat16)

        return carry

    lax.fori_loop(0, rows, one_row, 0)


def give_back(steps, order, tok_count, at, places, adapters_here, table, grad_down, grad_up):
    block_count, rank, wide = grad_down.shape
    narrow = grad_up.shape[2]
    vmem = pl.BlockSpec(memory_space=pltpu.VMEM)
    smem = pl.BlockSpec(memory_space=pltpu.SMEM)
    slots = (steps * CUTS, rank // CUTS, wide + narrow)
    row_step = math.gcd(adapters_here, 8)
    from_left, from_right = pl.pallas_call(
        functools.partial(back_kernel, tok_count, steps, at),
        out_shape=(jax.ShapeDtypeStruct(slots, jnp.bfloat16),) * 2,
        in_specs=[smem, vmem, vmem],
        out_specs=(vmem, vmem),
        scratch_shapes=[pltpu.VMEM(slots, jnp.bfloat16)] * 2
        + [pltpu.SemaphoreType.DMA((2, steps * CUTS))] * 2,
        compiler_params=pltpu.CompilerParams(
            collective_id=order, has_side_effects=True, vmem_limit_bytes=VMEM_LIMIT
        ),
        name="return_grads",
    )(
        table,
        grad_down.reshape(-1, rank // CUTS, wide),
        grad_up.reshape(-1, rank // CUTS, narrow),
    )
    from_left = from_left.reshape(steps, rank, wide + narrow)
    from_right = from_right.reshape(steps, rank, wide + narrow)
    return pl.pallas_call(
        functools.partial(sum_kernel, at, places, block_count),
        grid=(adapters_here // row_step,),
        out_shape=(
            jax.ShapeDtypeStruct((adapters_here, rank, wide), jnp.bfloat16),
            jax.ShapeDtypeStruct((adapters_here, rank, narrow), jnp.bfloat16),
        ),
        in_specs=[smem, vmem, vmem, vmem, vmem],
        out_specs=(
            pl.BlockSpec((row_step, rank, wide), lambda i: (i, 0, 0)),
            pl.BlockSpec((row_step, rank, narrow), lambda i: (i, 0, 0)),
        ),
        scratch_shapes=[
            pltpu.VMEM((rank, wide), jnp.float32),
            pltpu.VMEM((rank, narrow), jnp.float32),
        ],
        compiler_params=pltpu.CompilerParams(vmem_limit_bytes=VMEM_LIMIT),
        name="sum_grads",
    )(table, grad_down, grad_up, from_left, from_right)


def middle_kernel(
    mp_count, sub_count, at, table, down, up, rows, base, teacher, grad_down, grad_up,
    acts_part, acts_in, acts, ranks_part, ranks_in, ranks, sum_down, sum_up, send_sem, recv_sem,
):
    block_count = down.shape[0]
    count = mp_count * sub_count
    share = block_count // count
    me = lax.axis_index("mp") * sub_count + lax.axis_index("sub")
    live = table[at["live"]]

    def device(k):
        peer = lax.rem(me + k, count)
        return peer, {"mp": lax.div(peer, sub_count), "sub": lax.rem(peer, sub_count)}

    barrier = pltpu.get_barrier_semaphore()
    for k in range(1, count):
        pl.semaphore_signal(barrier, inc=1, device_id=device(k)[1])

    def token_rows(j):
        return pl.ds(pl.multiple_of(j * BLK, BLK), BLK)

    def scatter(phase, k, part, landing):
        peer, target = device(k)
        return pltpu.make_async_remote_copy(
            src_ref=part.at[pl.ds(peer * share, share)],
            dst_ref=landing.at[k],
            send_sem=send_sem.at[phase, k],
            recv_sem=recv_sem.at[phase, k],
            device_id=target,
        )

    def spread(phase, k, full):
        _, target = device(k)
        mine = pl.ds(me * share, share)
        return pltpu.make_async_remote_copy(
            src_ref=full.at[mine],
            dst_ref=full.at[mine],
            send_sem=send_sem.at[phase, k],
            recv_sem=recv_sem.at[phase, k],
            device_id=target,
        )

    def total(phase, part, landing, full):
        for k in range(1, count):
            scatter(phase, k, part, landing).wait()
        mine = pl.ds(me * share, share)
        value = part[mine].astype(jnp.float32)
        for k in range(1, count):
            value += landing[k].astype(jnp.float32)
        full[mine] = value.astype(jnp.bfloat16)
        for k in range(1, count):
            spread(phase + 1, k, full).start()
        for k in range(1, count):
            spread(phase + 1, k, full).wait()

    def act(j):
        acts_part[j] = lax.dot_general(
            down[j], rows[token_rows(j), :], (((1,), (1,)), ((), ())),
            preferred_element_type=jnp.float32,
        ).astype(jnp.bfloat16)

    def quarters(compute, phase, part, landing):
        for k in list(range(1, count)) + [0]:
            peer, _ = device(k)

            def one(i, carry):
                compute(peer * share + i)
                return carry

            lax.fori_loop(0, share, one, 0, unroll=True)
            if k == 1 and phase == 0:
                pl.semaphore_wait(barrier, count - 1)
            if k:
                scatter(phase, k, part, landing).start()

    quarters(act, 0, acts_part, acts_in)
    total(0, acts_part, acts_in, acts)

    def residual(j):
        delta = lax.dot_general(
            acts[j], up[j], (((0,), (0,)), ((), ())), preferred_element_type=jnp.float32
        )
        frozen = base[:, token_rows(j)].astype(jnp.float32).T
        error = frozen + adapter_scale * delta - teacher[token_rows(j), :].astype(jnp.float32)
        error = jnp.where(j < live, error, 0.0)
        out_grad = (error / BLK).astype(jnp.bfloat16)
        sum_up[j] = adapter_scale * jnp.dot(
            acts[j], out_grad, preferred_element_type=jnp.float32
        )
        ranks_part[j] = (
            adapter_scale
            * lax.dot_general(
                up[j], out_grad, (((1,), (1,)), ((), ())), preferred_element_type=jnp.float32
            )
        ).astype(jnp.bfloat16)

    quarters(residual, 2, ranks_part, ranks_in)
    total(2, ranks_part, ranks_in, ranks)

    for j in reversed(range(block_count)):
        term = jnp.dot(ranks[j], rows[j * BLK:(j + 1) * BLK, :], preferred_element_type=jnp.float32)
        term_up = sum_up[j]
        if j < block_count - 1:
            after = table[at["again"] + j]
            other = jnp.maximum(after, j + 1)
            term = term + jnp.where(after >= 0, sum_down[other], 0.0)
            term_up = term_up + jnp.where(after >= 0, sum_up[other], 0.0)
            sum_up[j] = term_up
        sum_down[j] = term
        grad_down[j] = term.astype(jnp.bfloat16)
        grad_up[j] = term_up.astype(jnp.bfloat16)


def middle(order, mp_count, sub_count, at, table, down, up, rows, base, teacher):
    block_count, rank, wide = down.shape
    narrow = up.shape[2]
    count = mp_count * sub_count
    vmem = pl.BlockSpec(memory_space=pltpu.VMEM)
    small = pltpu.VMEM((block_count, rank, BLK), jnp.bfloat16)
    landing = pltpu.VMEM((count, block_count // count, rank, BLK), jnp.bfloat16)
    return pl.pallas_call(
        functools.partial(middle_kernel, mp_count, sub_count, at),
        out_shape=(
            jax.ShapeDtypeStruct((block_count, rank, wide), jnp.bfloat16),
            jax.ShapeDtypeStruct((block_count, rank, narrow), jnp.bfloat16),
        ),
        in_specs=[pl.BlockSpec(memory_space=pltpu.SMEM)] + [vmem] * 5,
        out_specs=(vmem, vmem),
        scratch_shapes=[
            small, landing, small, small, landing, small,
            pltpu.VMEM((block_count, rank, wide), jnp.float32),
            pltpu.VMEM((block_count, rank, narrow), jnp.float32),
            pltpu.SemaphoreType.DMA((4, count)),
            pltpu.SemaphoreType.DMA((4, count)),
        ],
        compiler_params=pltpu.CompilerParams(
            collective_id=order, has_side_effects=True, vmem_limit_bytes=VMEM_LIMIT
        ),
        name="middle",
    )(table, down, up, rows, base, teacher)


def on_device(inputs, base_weight, panel_a, panel_b, teacher, block_ids, home_rows, live_blocks):
    width_piece = inputs.shape[1]
    block_count = inputs.shape[0] // BLK
    tok_count = lax.axis_size("tok")
    capacity = max(1, 2 * block_count // tok_count)
    adapters_here, rank_width, _ = panel_a.shape
    col_width = panel_b.shape[2]
    mp_count, sub_count = lax.axis_size("mp"), lax.axis_size("sub")
    places = capacity * (tok_count // 2) * (tok_count - tok_count // 2)
    slot_bytes = 2 * rank_width * (width_piece + col_width)
    if 4 * places * slot_bytes > 24 * MIB or block_count % (mp_count * sub_count):
        return padded_exchange(
            inputs, base_weight, panel_a, panel_b, teacher, block_ids, home_rows, live_blocks
        )
    at, _ = table_layout(places, block_count, adapters_here)
    table = make_table(block_ids, home_rows, live_blocks, adapters_here, places)
    needed = table[at["count"]:at["count"] + 1]
    groups = lax.axis_size("groups")
    most = needed
    for shift in range(1, groups):
        other = lax.ppermute(needed, "groups", [(g, (g + shift) % groups) for g in range(groups)])
        most = jnp.maximum(most, other)
    steps_list = [s for s in STEPS if s < places] + [places]
    branch = jnp.sum(most[0] > jnp.array(steps_list[:-1], jnp.int32)).astype(jnp.int32)

    base_rows = lax.psum_scatter(
        lax.dot_general(
            base_weight, inputs, (((0,), (1,)), ((), ())), preferred_element_type=jnp.float32
        ).astype(jnp.bfloat16),
        ("mp", "sub"),
        scatter_dimension=0,
        tiled=True,
    )

    block_down, block_up = lax.switch(
        branch,
        [
            functools.partial(
                lambda steps, order, t, a, b: fetch(
                    steps, order, tok_count, at, t, a, b, block_count
                ),
                steps,
                order,
            )
            for order, steps in enumerate(steps_list)
        ],
        table,
        panel_a,
        panel_b,
    )
    grad_down, grad_up = middle(
        2 * len(steps_list), mp_count, sub_count, at, table, block_down, block_up, inputs,
        base_rows, teacher,
    )
    return lax.switch(
        branch,
        [
            functools.partial(
                lambda steps, order, t, a, b: give_back(
                    steps, order, tok_count, at, places, adapters_here, t, a, b
                ),
                steps,
                len(steps_list) + order,
            )
            for order, steps in enumerate(steps_list)
        ],
        table,
        grad_down,
        grad_up,
    )


def solution(mesh):
    placed = (
        P(("groups", "tok"), ("mp", "sub")),
        P(("mp", "sub"), None),
        P(("groups", "tok"), None, ("mp", "sub")),
        P(("groups", "tok"), None, ("mp", "sub")),
        P(("groups", "tok"), ("mp", "sub")),
        P("groups", None),
        P("groups"),
        P("groups"),
    )
    return jax.shard_map(
        on_device,
        mesh=mesh,
        in_specs=placed,
        out_specs=(
            P(("groups", "tok"), None, ("mp", "sub")),
            P(("groups", "tok"), None, ("mp", "sub")),
        ),
        check_vma=False,
    )
```

```python
import jax
import jax.numpy as jnp
import functools
import math

from jax import lax
from jax.experimental import pallas as pl
from jax.experimental.pallas import tpu as pltpu
from jax.sharding import PartitionSpec as P

BLK = 128


adapter_scale = 2.0


def padded_exchange(inputs, base_weight, panel_a, panel_b, teacher, block_ids, home_rows, live_blocks):
    width_piece = inputs.shape[1]
    block_count = inputs.shape[0] // BLK
    tok_count = lax.axis_size("tok")
    own_index = lax.axis_index("tok")
    capacity = max(1, 2 * block_count // tok_count)
    slot_total = tok_count * capacity
    adapters_here = panel_a.shape[0]
    rank_width = panel_a.shape[1]
    col_width = panel_b.shape[2]
    slot_all = home_rows[block_ids]
    owner_all = slot_all // adapters_here
    local_all = slot_all % adapters_here
    earlier = jnp.arange(block_count)[None, :] < jnp.arange(block_count)[:, None]
    same_owner = owner_all[:, :, None] == owner_all[:, None, :]
    rank_all = jnp.sum(same_owner & earlier[None], axis=2)
    place_all = owner_all * capacity + rank_all
    owned_here = owner_all == own_index
    owner_table = (
        owned_here[:, :, None, None]
        & (rank_all[:, :, None, None] == jnp.arange(capacity)[None, None, :, None])
        & (local_all[:, :, None, None] == jnp.arange(adapters_here)[None, None, None, :])
    )
    owner_table = (
        jnp.sum(owner_table, axis=1).reshape(slot_total, adapters_here).astype(jnp.float32)
    )
    place_here = lax.dynamic_index_in_dim(place_all, own_index, 0, keepdims=False)
    take_slots = (place_here[:, None] == jnp.arange(slot_total)[None, :]).astype(jnp.float32)
    live_here = lax.dynamic_index_in_dim(live_blocks, own_index, 0, keepdims=False)
    active_row_list = (jnp.arange(block_count) < live_here).astype(jnp.float32)[:, None, None]
    base_rows = lax.psum_scatter(
        lax.dot_general(
            base_weight, inputs, (((0,), (1,)), ((), ())), preferred_element_type=jnp.float32
        ).astype(jnp.bfloat16),
        ("mp", "sub"),
        scatter_dimension=0,
        tiled=True,
    ).astype(jnp.float32)
    frozen_base_output = base_rows.T.reshape(block_count, BLK, col_width)
    teacher_output = teacher.reshape(block_count, BLK, col_width).astype(jnp.float32)
    row_blocks = inputs.reshape(block_count, BLK, width_piece)
    down_flat = panel_a.reshape(adapters_here, rank_width * width_piece)
    up_flat = panel_b.reshape(adapters_here, rank_width * col_width)
    table_low = owner_table.astype(jnp.bfloat16)
    slots_low = take_slots.astype(jnp.bfloat16)
    slot_down = jnp.dot(table_low, down_flat, preferred_element_type=jnp.float32).astype(
        jnp.bfloat16
    )
    slot_up = jnp.dot(table_low, up_flat, preferred_element_type=jnp.float32).astype(jnp.bfloat16)

    def collect(grads):
        summed = jnp.dot(
            owner_table.T,
            grads.reshape(slot_total, -1),
            precision=lax.Precision.HIGHEST,
            preferred_element_type=jnp.float32,
        )
        return summed

    sent_down = slot_down.reshape(tok_count, capacity, -1)
    sent_up = slot_up.reshape(tok_count, capacity, -1)
    got_down, got_up = (
        lax.all_to_all(sent_down, "tok", split_axis=0, concat_axis=0, tiled=True),
        lax.all_to_all(sent_up, "tok", split_axis=0, concat_axis=0, tiled=True),
    )
    block_down = jnp.dot(
        slots_low, got_down.reshape(slot_total, -1), preferred_element_type=jnp.float32
    )
    block_down = block_down.astype(jnp.bfloat16).reshape(block_count, rank_width, width_piece)
    block_up = jnp.dot(
        slots_low, got_up.reshape(slot_total, -1), preferred_element_type=jnp.float32
    )
    block_up = block_up.astype(jnp.bfloat16).reshape(block_count, rank_width, col_width)
    acts_part = jnp.einsum(
        "jrd,jtd->jrt", block_down, row_blocks, preferred_element_type=jnp.float32
    )
    rank_activations = lax.psum(acts_part.astype(jnp.bfloat16), ("mp", "sub"))
    adapter_delta_output = jnp.einsum(
        "jrt,jrc->jtc", rank_activations, block_up, preferred_element_type=jnp.float32
    )
    student_error = (
        frozen_base_output + adapter_scale * adapter_delta_output - teacher_output
    ) * active_row_list
    output_gradient_rows = (student_error / BLK).astype(jnp.bfloat16)
    up_weight_gradient = adapter_scale * jnp.einsum(
        "jrt,jtc->jrc", rank_activations, output_gradient_rows, preferred_element_type=jnp.float32
    )
    partial_gradient_sums = adapter_scale * jnp.einsum(
        "jtc,jrc->jrt", output_gradient_rows, block_up, preferred_element_type=jnp.float32
    )
    rank_gradient_rows = lax.psum(partial_gradient_sums.astype(jnp.bfloat16), ("mp", "sub"))
    grad_down = jnp.einsum(
        "jrt,jtd->jrd", rank_gradient_rows, row_blocks, preferred_element_type=jnp.float32
    )
    back_down = jnp.dot(
        take_slots.T,
        grad_down.reshape(block_count, -1),
        precision=lax.Precision.HIGHEST,
        preferred_element_type=jnp.float32,
    ).reshape(tok_count, capacity, -1)
    back_up = jnp.dot(
        take_slots.T,
        up_weight_gradient.reshape(block_count, -1),
        precision=lax.Precision.HIGHEST,
        preferred_element_type=jnp.float32,
    ).reshape(tok_count, capacity, -1)
    held_down, held_up = (
        lax.all_to_all(
            back_down.astype(jnp.bfloat16), "tok", split_axis=0, concat_axis=0, tiled=True
        ).astype(back_down.dtype),
        lax.all_to_all(
            back_up.astype(jnp.bfloat16), "tok", split_axis=0, concat_axis=0, tiled=True
        ).astype(back_up.dtype),
    )
    grad_a = collect(held_down)
    grad_b = collect(held_up)
    grad_a = grad_a.reshape(adapters_here, rank_width, width_piece).astype(jnp.bfloat16)
    grad_b = grad_b.reshape(adapters_here, rank_width, col_width).astype(jnp.bfloat16)
    return (grad_a, grad_b)


STEPS = (9, 10, 11, 12, 13, 14, 15, 17, 20)
SKEW = 4
CUTS = 2
MIB = 1024 * 1024
VMEM_LIMIT = 56 * MIB


def table_layout(places, block_count, adapters_here):
    sizes = dict(
        out_right=places,
        out_left=places,
        back_right=places,
        back_left=places,
        kind=block_count,
        source=block_count,
        head=adapters_here,
        chain=block_count + 2 * places,
        again=block_count,
        live=1,
        count=1,
    )
    at, offset = {}, 0
    for name, size in sizes.items():
        at[name] = offset
        offset += size
    return at, offset


def table_kernel(tok_count, block_count, adapters_here, places, ids, home, live, table, slot, free, items, seen, first_of
):
    at, total = table_layout(places, block_count, adapters_here)
    me = lax.axis_index("tok")

    def clear(i, carry):
        table[i] = jnp.int32(-1)
        return carry

    lax.fori_loop(0, total, clear, 0, unroll=8)

    def forget(i, carry):
        seen[i] = jnp.int32(-1)
        return carry

    lax.fori_loop(0, tok_count * adapters_here, forget, 0, unroll=8)
    table[at["live"]] = live[me]

    def look_up(i, carry):
        t, j = lax.div(i, block_count), lax.rem(i, block_count)
        row = home[ids[t, j]]
        alive = j < live[t]
        before = seen[row]
        twin = alive & (before >= t * block_count)
        slot[i] = jnp.where(alive & jnp.logical_not(twin), row, -1)
        first_of[i] = jnp.where(twin, first_of[jnp.maximum(before, 0)], i)

        @pl.when(alive)
        def _():
            seen[row] = i

        @pl.when(twin & (t == me))
        def _():
            table[at["again"] + lax.rem(before, block_count)] = j

        return carry

    lax.fori_loop(0, tok_count * block_count, look_up, 0, unroll=4)

    def own(j, carry):
        table[at["kind"] + j] = jnp.int32(0)
        table[at["source"] + j] = jnp.int32(0)
        row = slot[me * block_count + j]
        local = row - me * adapters_here

        @pl.when((row >= 0) & (local >= 0) & (local < adapters_here))
        def _():
            table[at["source"] + j] = local
            table[at["chain"] + j] = table[at["head"] + local]
            table[at["head"] + local] = j

        return carry

    lax.fori_loop(0, block_count, own, 0)

    used = jnp.int32(0)
    for right in (True, False):

        def reset(p, carry):
            free[p] = jnp.int32(0 if right else tok_count - 1)
            return carry

        lax.fori_loop(0, places, reset, 0, unroll=8)
        owners = range(tok_count - 1) if right else range(tok_count - 1, 0, -1)
        for s in owners:
            first, last = (s + 1, tok_count) if right else (0, s)

            def gather(i, n):
                row = slot[i]
                hit = (row >= s * adapters_here) & (row < (s + 1) * adapters_here)

                @pl.when(hit)
                def _():
                    items[n] = i

                return n + hit.astype(jnp.int32)

            n = lax.fori_loop(
                first * block_count, last * block_count, gather, jnp.int32(0), unroll=4
            )

            def assign(p, carry):
                k, most = carry
                ok = (free[p] <= s) if right else (free[p] >= s)
                ok = ok & (k < n)

                @pl.when(ok)
                def _():
                    i = items[k]
                    d, j = lax.div(i, block_count), lax.rem(i, block_count)
                    local = slot[i] - s * adapters_here
                    free[p] = d

                    @pl.when(me == s)
                    def _():
                        table[at["out_right" if right else "out_left"] + p] = local
                        item = block_count + p + (places if right else 0)
                        table[at["chain"] + item] = table[at["head"] + local]
                        table[at["head"] + local] = item

                    @pl.when(me == d)
                    def _():
                        table[at["kind"] + j] = jnp.int32(1 if right else 2)
                        table[at["source"] + j] = p
                        table[at["back_left" if right else "back_right"] + p] = j

                return (k + ok.astype(jnp.int32), jnp.where(ok, jnp.maximum(most, p + 1), most))

            _, used = lax.fori_loop(0, places, assign, (jnp.int32(0), used), unroll=4)
    table[at["count"]] = used

    def share(j, carry):
        first = lax.rem(first_of[me * block_count + j], block_count)
        table[at["kind"] + j] = table[at["kind"] + first]
        table[at["source"] + j] = table[at["source"] + first]
        return carry

    lax.fori_loop(0, block_count, share, 0)


def make_table(block_ids, home_rows, live_blocks, adapters_here, places):
    tok_count, block_count = block_ids.shape
    _, total = table_layout(places, block_count, adapters_here)
    smem = pl.BlockSpec(memory_space=pltpu.SMEM)
    return pl.pallas_call(
        functools.partial(table_kernel, tok_count, block_count, adapters_here, places),
        out_shape=jax.ShapeDtypeStruct((total,), jnp.int32),
        in_specs=[smem] * 3,
        out_specs=smem,
        scratch_shapes=[
            pltpu.SMEM((tok_count * block_count,), jnp.int32),
            pltpu.SMEM((places,), jnp.int32),
            pltpu.SMEM((tok_count * block_count,), jnp.int32),
            pltpu.SMEM((tok_count * adapters_here,), jnp.int32),
            pltpu.SMEM((tok_count * block_count,), jnp.int32),
        ],
        name="place_table",
    )(block_ids, home_rows, live_blocks)


def run_belts(
    tok_count, steps, at_right, at_left, table, wide, narrow,
    from_left, from_right, to_right, to_left, send_sem, recv_sem,
):
    me = lax.axis_index("tok")
    split = wide.shape[2]
    barrier = pltpu.get_barrier_semaphore()

    @pl.when(me > 0)
    def _():
        pl.semaphore_signal(barrier, inc=1, device_id={"tok": me - 1})

    @pl.when(me < tok_count - 1)
    def _():
        pl.semaphore_signal(barrier, inc=1, device_id={"tok": me + 1})

    @pl.when((me == 0) | (me == tok_count - 1))
    def _():
        pl.semaphore_wait(barrier, 1)

    @pl.when((me > 0) & (me < tok_count - 1))
    def _():
        pl.semaphore_wait(barrier, 2)

    def copy(belt, p, target):
        outgoing, incoming = (to_right, from_left) if belt == 0 else (to_left, from_right)
        return pltpu.make_async_remote_copy(
            src_ref=outgoing.at[p],
            dst_ref=incoming.at[p],
            send_sem=send_sem.at[belt, p],
            recv_sem=recv_sem.at[belt, p],
            device_id={"tok": target},
        )

    def belt_step(belt, p):
        position = me if belt == 0 else tok_count - 1 - me
        target = me + 1 if belt == 0 else me - 1
        outgoing, incoming = (to_right, from_left) if belt == 0 else (to_left, from_right)
        at = at_right if belt == 0 else at_left
        inside = (p >= 0) & (p < steps * CUTS)

        @pl.when(inside & (position > 0))
        def _():
            copy(belt, p, target).wait_recv()

        @pl.when(inside & (position == 0))
        def _():
            own = jnp.maximum(table[at + lax.div(p, CUTS)], 0) * CUTS + lax.rem(p, CUTS)
            outgoing[p, :, :split] = wide[own]
            outgoing[p, :, split:] = narrow[own]

        @pl.when(inside & (position > 0) & (position < tok_count - 1))
        def _():
            own = table[at + lax.div(p, CUTS)]
            fresh = own >= 0
            own = jnp.maximum(own, 0) * CUTS + lax.rem(p, CUTS)
            outgoing[p, :, :split] = jnp.where(fresh, wide[own], incoming[p, :, :split])
            outgoing[p, :, split:] = jnp.where(fresh, narrow[own], incoming[p, :, split:])

        @pl.when(inside & (position < tok_count - 1))
        def _():
            copy(belt, p, target).start()

    def one_round(r, carry):
        belt_step(0, r - SKEW * me)
        belt_step(1, r - SKEW * (tok_count - 1 - me))
        return carry

    lax.fori_loop(0, steps * CUTS + SKEW * (tok_count - 1), one_round, 0)

    def finish(p, carry):
        @pl.when(me < tok_count - 1)
        def _():
            copy(0, p, me + 1).wait_send()

        @pl.when(me > 0)
        def _():
            copy(1, p, me - 1).wait_send()

        return carry

    lax.fori_loop(0, steps * CUTS, finish, 0)


def out_kernel(
    tok_count, steps, at, table, panel_a, panel_b, down, up,
    from_left, from_right, to_right, to_left, send_sem, recv_sem,
):
    run_belts(
        tok_count, steps, at["out_right"], at["out_left"], table, panel_a, panel_b,
        from_left, from_right, to_right, to_left, send_sem, recv_sem,
    )
    split = panel_a.shape[2]

    def pick(j, carry):
        block, cut = lax.div(j, CUTS), lax.rem(j, CUTS)
        kind = table[at["kind"] + block]
        source = table[at["source"] + block] * CUTS + cut
        own = jnp.where(kind == 0, source, 0)
        left = jnp.where(kind == 1, source, 0)
        right = jnp.where(kind == 2, source, 0)
        down[j] = jnp.where(
            kind == 0,
            panel_a[own],
            jnp.where(kind == 1, from_left[left, :, :split], from_right[right, :, :split]),
        )
        up[j] = jnp.where(
            kind == 0,
            panel_b[own],
            jnp.where(kind == 1, from_left[left, :, split:], from_right[right, :, split:]),
        )
        return carry

    lax.fori_loop(0, down.shape[0], pick, 0)


def fetch(steps, order, tok_count, at, table, panel_a, panel_b, block_count):
    rank, wide = panel_a.shape[1:]
    narrow = panel_b.shape[2]
    vmem = pl.BlockSpec(memory_space=pltpu.VMEM)
    slots = pltpu.VMEM((steps * CUTS, rank // CUTS, wide + narrow), jnp.bfloat16)
    down, up = pl.pallas_call(
        functools.partial(out_kernel, tok_count, steps, at),
        out_shape=(
            jax.ShapeDtypeStruct((block_count * CUTS, rank // CUTS, wide), jnp.bfloat16),
            jax.ShapeDtypeStruct((block_count * CUTS, rank // CUTS, narrow), jnp.bfloat16),
        ),
        in_specs=[pl.BlockSpec(memory_space=pltpu.SMEM), vmem, vmem],
        out_specs=(vmem, vmem),
        scratch_shapes=[slots] * 4
        + [pltpu.SemaphoreType.DMA((2, steps * CUTS))] * 2,
        compiler_params=pltpu.CompilerParams(
            collective_id=order, has_side_effects=True, vmem_limit_bytes=VMEM_LIMIT
        ),
        name="fetch_panels",
    )(table, panel_a.reshape(-1, rank // CUTS, wide), panel_b.reshape(-1, rank // CUTS, narrow))
    return down.reshape(block_count, rank, wide), up.reshape(block_count, rank, narrow)


def back_kernel(
    tok_count, steps, at, table, grad_down, grad_up, from_left, from_right,
    to_right, to_left, send_sem, recv_sem,
):
    run_belts(
        tok_count, steps, at["back_right"], at["back_left"], table, grad_down, grad_up,
        from_left, from_right, to_right, to_left, send_sem, recv_sem,
    )


def sum_kernel(
    at, places, block_count, table, grad_down, grad_up, from_left, from_right, grad_a, grad_b,
    sum_a, sum_b,
):
    split = grad_down.shape[2]
    rows = grad_a.shape[0]
    first = pl.program_id(0) * rows

    def one_row(i, carry):
        head = table[at["head"] + first + i]

        @pl.when(head < 0)
        def _():
            grad_a[i] = jnp.zeros(grad_a.shape[1:], jnp.bfloat16)
            grad_b[i] = jnp.zeros(grad_b.shape[1:], jnp.bfloat16)

        @pl.when(head >= 0)
        def _():
            sum_a[...] = jnp.zeros_like(sum_a)
            sum_b[...] = jnp.zeros_like(sum_b)

            def step(item):
                belt = item - block_count

                @pl.when(belt < 0)
                def _():
                    sum_a[...] += grad_down[item].astype(jnp.float32)
                    sum_b[...] += grad_up[item].astype(jnp.float32)

                @pl.when((belt >= 0) & (belt < places))
                def _():
                    sum_a[...] += from_left[belt, :, :split].astype(jnp.float32)
                    sum_b[...] += from_left[belt, :, split:].astype(jnp.float32)

                @pl.when(belt >= places)
                def _():
                    sum_a[...] += from_right[belt - places, :, :split].astype(jnp.float32)
                    sum_b[...] += from_right[belt - places, :, split:].astype(jnp.float32)

                return table[at["chain"] + item]

            lax.while_loop(lambda item: item >= 0, step, head)
            grad_a[i] = sum_a[...].astype(jnp.bfloat16)
            grad_b[i] = sum_b[...].astype(jnp.bfloat16)

        return carry

    lax.fori_loop(0, rows, one_row, 0)


def give_back(steps, order, tok_count, at, places, adapters_here, table, grad_down, grad_up):
    block_count, rank, wide = grad_down.shape
    narrow = grad_up.shape[2]
    vmem = pl.BlockSpec(memory_space=pltpu.VMEM)
    smem = pl.BlockSpec(memory_space=pltpu.SMEM)
    slots = (steps * CUTS, rank // CUTS, wide + narrow)
    row_step = math.gcd(adapters_here, 8)
    from_left, from_right = pl.pallas_call(
        functools.partial(back_kernel, tok_count, steps, at),
        out_shape=(jax.ShapeDtypeStruct(slots, jnp.bfloat16),) * 2,
        in_specs=[smem, vmem, vmem],
        out_specs=(vmem, vmem),
        scratch_shapes=[pltpu.VMEM(slots, jnp.bfloat16)] * 2
        + [pltpu.SemaphoreType.DMA((2, steps * CUTS))] * 2,
        compiler_params=pltpu.CompilerParams(
            collective_id=order, has_side_effects=True, vmem_limit_bytes=VMEM_LIMIT
        ),
        name="return_grads",
    )(
        table,
        grad_down.reshape(-1, rank // CUTS, wide),
        grad_up.reshape(-1, rank // CUTS, narrow),
    )
    from_left = from_left.reshape(steps, rank, wide + narrow)
    from_right = from_right.reshape(steps, rank, wide + narrow)
    return pl.pallas_call(
        functools.partial(sum_kernel, at, places, block_count),
        grid=(adapters_here // row_step,),
        out_shape=(
            jax.ShapeDtypeStruct((adapters_here, rank, wide), jnp.bfloat16),
            jax.ShapeDtypeStruct((adapters_here, rank, narrow), jnp.bfloat16),
        ),
        in_specs=[smem, vmem, vmem, vmem, vmem],
        out_specs=(
            pl.BlockSpec((row_step, rank, wide), lambda i: (i, 0, 0)),
            pl.BlockSpec((row_step, rank, narrow), lambda i: (i, 0, 0)),
        ),
        scratch_shapes=[
            pltpu.VMEM((rank, wide), jnp.float32),
            pltpu.VMEM((rank, narrow), jnp.float32),
        ],
        compiler_params=pltpu.CompilerParams(vmem_limit_bytes=VMEM_LIMIT),
        name="sum_grads",
    )(table, grad_down, grad_up, from_left, from_right)


def middle_kernel(
    mp_count, sub_count, at, table, down, up, rows, base, teacher, grad_down, grad_up,
    acts_part, acts_in, acts, ranks_part, ranks_in, ranks, sum_down, sum_up, send_sem, recv_sem,
):
    block_count = down.shape[0]
    count = mp_count * sub_count
    share = block_count // count
    me = lax.axis_index("mp") * sub_count + lax.axis_index("sub")
    live = table[at["live"]]

    def device(k):
        peer = lax.rem(me + k, count)
        return peer, {"mp": lax.div(peer, sub_count), "sub": lax.rem(peer, sub_count)}

    barrier = pltpu.get_barrier_semaphore()
    for k in range(1, count):
        pl.semaphore_signal(barrier, inc=1, device_id=device(k)[1])

    def token_rows(j):
        return pl.ds(pl.multiple_of(j * BLK, BLK), BLK)

    def scatter(phase, k, part, landing):
        peer, target = device(k)
        return pltpu.make_async_remote_copy(
            src_ref=part.at[pl.ds(peer * share, share)],
            dst_ref=landing.at[k],
            send_sem=send_sem.at[phase, k],
            recv_sem=recv_sem.at[phase, k],
            device_id=target,
        )

    def spread(phase, k, full):
        _, target = device(k)
        mine = pl.ds(me * share, share)
        return pltpu.make_async_remote_copy(
            src_ref=full.at[mine],
            dst_ref=full.at[mine],
            send_sem=send_sem.at[phase, k],
            recv_sem=recv_sem.at[phase, k],
            device_id=target,
        )

    def total(phase, part, landing, full):
        for k in range(1, count):
            scatter(phase, k, part, landing).wait()
        mine = pl.ds(me * share, share)
        value = part[mine].astype(jnp.float32)
        for k in range(1, count):
            value += landing[k].astype(jnp.float32)
        full[mine] = value.astype(jnp.bfloat16)
        for k in range(1, count):
            spread(phase + 1, k, full).start()
        for k in range(1, count):
            spread(phase + 1, k, full).wait()

    def act(j):
        acts_part[j] = lax.dot_general(
            down[j], rows[token_rows(j), :], (((1,), (1,)), ((), ())),
            preferred_element_type=jnp.float32,
        ).astype(jnp.bfloat16)

    def quarters(compute, phase, part, landing):
        for k in list(range(1, count)) + [0]:
            peer, _ = device(k)

            def one(i, carry):
                compute(peer * share + i)
                return carry

            lax.fori_loop(0, share, one, 0, unroll=True)
            if k == 1 and phase == 0:
                pl.semaphore_wait(barrier, count - 1)
            if k:
                scatter(phase, k, part, landing).start()

    quarters(act, 0, acts_part, acts_in)
    total(0, acts_part, acts_in, acts)

    def residual(j):
        delta = lax.dot_general(
            acts[j], up[j], (((0,), (0,)), ((), ())), preferred_element_type=jnp.float32
        )
        frozen = base[:, token_rows(j)].astype(jnp.float32).T
        error = frozen + adapter_scale * delta - teacher[token_rows(j), :].astype(jnp.float32)
        error = jnp.where(j < live, error, 0.0)
        out_grad = (error / BLK).astype(jnp.bfloat16)
        sum_up[j] = adapter_scale * jnp.dot(
            acts[j], out_grad, preferred_element_type=jnp.float32
        )
        ranks_part[j] = (
            adapter_scale
            * lax.dot_general(
                up[j], out_grad, (((1,), (1,)), ((), ())), preferred_element_type=jnp.float32
            )
        ).astype(jnp.bfloat16)

    quarters(residual, 2, ranks_part, ranks_in)
    total(2, ranks_part, ranks_in, ranks)

    for j in reversed(range(block_count)):
        term = jnp.dot(ranks[j], rows[j * BLK:(j + 1) * BLK, :], preferred_element_type=jnp.float32)
        term_up = sum_up[j]
        if j < block_count - 1:
            after = table[at["again"] + j]
            other = jnp.maximum(after, j + 1)
            term = term + jnp.where(after >= 0, sum_down[other], 0.0)
            term_up = term_up + jnp.where(after >= 0, sum_up[other], 0.0)
            sum_up[j] = term_up
        sum_down[j] = term
        grad_down[j] = term.astype(jnp.bfloat16)
        grad_up[j] = term_up.astype(jnp.bfloat16)


def middle(order, mp_count, sub_count, at, table, down, up, rows, base, teacher):
    block_count, rank, wide = down.shape
    narrow = up.shape[2]
    count = mp_count * sub_count
    vmem = pl.BlockSpec(memory_space=pltpu.VMEM)
    small = pltpu.VMEM((block_count, rank, BLK), jnp.bfloat16)
    landing = pltpu.VMEM((count, block_count // count, rank, BLK), jnp.bfloat16)
    return pl.pallas_call(
        functools.partial(middle_kernel, mp_count, sub_count, at),
        out_shape=(
            jax.ShapeDtypeStruct((block_count, rank, wide), jnp.bfloat16),
            jax.ShapeDtypeStruct((block_count, rank, narrow), jnp.bfloat16),
        ),
        in_specs=[pl.BlockSpec(memory_space=pltpu.SMEM)] + [vmem] * 5,
        out_specs=(vmem, vmem),
        scratch_shapes=[
            small, landing, small, small, landing, small,
            pltpu.VMEM((block_count, rank, wide), jnp.float32),
            pltpu.VMEM((block_count, rank, narrow), jnp.float32),
            pltpu.SemaphoreType.DMA((4, count)),
            pltpu.SemaphoreType.DMA((4, count)),
        ],
        compiler_params=pltpu.CompilerParams(
            collective_id=order, has_side_effects=True, vmem_limit_bytes=VMEM_LIMIT
        ),
        name="middle",
    )(table, down, up, rows, base, teacher)


def on_device(inputs, base_weight, panel_a, panel_b, teacher, block_ids, home_rows, live_blocks):
    width_piece = inputs.shape[1]
    block_count = inputs.shape[0] // BLK
    tok_count = lax.axis_size("tok")
    capacity = max(1, 2 * block_count // tok_count)
    adapters_here, rank_width, _ = panel_a.shape
    col_width = panel_b.shape[2]
    mp_count, sub_count = lax.axis_size("mp"), lax.axis_size("sub")
    places = capacity * (tok_count // 2) * (tok_count - tok_count // 2)
    slot_bytes = 2 * rank_width * (width_piece + col_width)
    if 4 * places * slot_bytes > 24 * MIB or block_count % (mp_count * sub_count):
        return padded_exchange(
            inputs, base_weight, panel_a, panel_b, teacher, block_ids, home_rows, live_blocks
        )
    at, _ = table_layout(places, block_count, adapters_here)
    table = make_table(block_ids, home_rows, live_blocks, adapters_here, places)
    needed = table[at["count"]:at["count"] + 1]
    weight_after, table, needed = lax.optimization_barrier((base_weight, table, needed))
    groups = lax.axis_size("groups")
    most = needed
    for shift in range(1, groups):
        other = lax.ppermute(needed, "groups", [(g, (g + shift) % groups) for g in range(groups)])
        most = jnp.maximum(most, other)
    steps_list = [s for s in STEPS if s < places] + [places]
    branch = jnp.sum(most[0] > jnp.array(steps_list[:-1], jnp.int32)).astype(jnp.int32)

    base_rows = lax.psum_scatter(
        lax.dot_general(
            weight_after, inputs, (((0,), (1,)), ((), ())), preferred_element_type=jnp.float32
        ).astype(jnp.bfloat16),
        ("mp", "sub"),
        scatter_dimension=0,
        tiled=True,
    )

    block_down, block_up = lax.switch(
        branch,
        [
            functools.partial(
                lambda steps, order, t, a, b: fetch(
                    steps, order, tok_count, at, t, a, b, block_count
                ),
                steps,
                order,
            )
            for order, steps in enumerate(steps_list)
        ],
        table,
        panel_a,
        panel_b,
    )
    grad_down, grad_up = middle(
        2 * len(steps_list), mp_count, sub_count, at, table, block_down, block_up, inputs,
        base_rows, teacher,
    )
    return lax.switch(
        branch,
        [
            functools.partial(
                lambda steps, order, t, a, b: give_back(
                    steps, order, tok_count, at, places, adapters_here, t, a, b
                ),
                steps,
                len(steps_list) + order,
            )
            for order, steps in enumerate(steps_list)
        ],
        table,
        grad_down,
        grad_up,
    )


def solution(mesh):
    placed = (
        P(("groups", "tok"), ("mp", "sub")),
        P(("mp", "sub"), None),
        P(("groups", "tok"), None, ("mp", "sub")),
        P(("groups", "tok"), None, ("mp", "sub")),
        P(("groups", "tok"), ("mp", "sub")),
        P("groups", None),
        P("groups"),
        P("groups"),
    )
    return jax.shard_map(
        on_device,
        mesh=mesh,
        in_specs=placed,
        out_specs=(
            P(("groups", "tok"), None, ("mp", "sub")),
            P(("groups", "tok"), None, ("mp", "sub")),
        ),
        check_vma=False,
    )
```
